32 devices in a mesh: pair: 2 (over x), grow: 4 (over y, core), gcol: 4 (over z).
Axes of the slice: x: 2, y: 2, z: 4, core: 2. Of those that a mesh axis runs over, the one named last changes fastest.
Arguments:
- pair_elements: bfloat16 [1792, 8192], P('pair', ('grow', 'gcol')), may hold values from -0.75 to 0.75
- coulomb_root: float32 [8192], replicated, may hold values from 0.25 to 1
Outputs:
- factored: float32 [8192, 8192], P('grow', ('gcol', 'pair'))
The draws below stay inside these ranges and needn't reach their ends.
All inputs are finite; a program needn't handle non-finite values.
Results may differ from the reference program's by a relative error of at most 0.0003.
Values may be sent and summed in bfloat16 or wider, within the bound.
A program may use at most 128 MiB of HBM per device.

```python
import math
import jax
import jax.numpy as jnp
from jax import lax

NG = 8192
PANEL = 512
PANELS = 2
NPAIR = 1792


def with_spikes(array, rng, source, target, parts, factor):
    owner, partner = [(jnp.arange(array.shape[position]) // (array.shape[position] // parts)).reshape([-1 if axis == position else 1 for axis in range(array.ndim)]) for position in (source, target)]
    chosen = jax.random.permutation(rng, parts)[partner]
    strong = (owner == chosen) | (owner == (partner + parts // 2) % parts)
    return jnp.where(strong, factor * array, array)


def block_levels(rng, extent, pieces, low, top_value):
    def one(axis_at, shards_of):
        draws = jax.random.uniform(jax.random.fold_in(jax.random.fold_in(rng, 6), axis_at), (shards_of,), jnp.float32, low / len(pieces), top_value / len(pieces))
        return jnp.repeat(jnp.exp(draws), extent[axis_at] // shards_of).reshape((-1,) + (1,) * (len(extent) - axis_at - 1))

    loudness = one(*pieces[0])
    for cut in pieces[1:]:
        loudness = loudness * one(*cut)
    return loudness


def heavy_noise(key, dims, width, limit, split, heavy, kind=jnp.bfloat16):
    array = width * jax.random.normal(key, dims, jnp.float32)
    if split:
        array = array * block_levels(key, dims, split, -0.22, 0.18)
    return jnp.clip(with_spikes(array, jax.random.fold_in(key, 3), *heavy), -limit, limit).astype(kind)


def setup_inputs(seed: int = 0) -> dict:
    keys = jax.random.split(jax.random.key(seed), 3)
    pair_elements = heavy_noise(keys[0], (NPAIR, NG), (NPAIR // 16) ** -0.5, 0.75, ((0, 2), (1, 16)), (0, 1, 16, 2.0))
    coulomb_root = jnp.clip(jnp.exp(jax.random.uniform(keys[1], (NG,), jnp.float32, math.log(0.25), math.log(1.0))), 0.25, 1.0)
    return {"pair_elements": pair_elements, "coulomb_root": coulomb_root}


def reference(pair_elements, coulomb_root):
    elements = pair_elements.astype(jnp.float32)
    chi = jnp.dot(elements.T, elements, precision=lax.Precision.HIGHEST)
    row_ids = jnp.arange(NG, dtype=jnp.int32)[:, None]
    col_ids = jnp.arange(NG, dtype=jnp.int32)[None, :]
    working = jnp.where(row_ids == col_ids, 1.0, 0.0).astype(jnp.float32) + coulomb_root[:, None] * chi * coulomb_root[None, :]
    packed = jnp.zeros((NG, NG), jnp.float32)
    covered = jnp.zeros((NG, NG), bool)
    for step_index in range(PANELS):
        first = step_index * PANEL
        panel_cols = working[:, first:first + PANEL]
        factor = jnp.linalg.cholesky(panel_cols[first:first + PANEL])
        low_full = lax.linalg.triangular_solve(factor, panel_cols, left_side=False, lower=True, transpose_a=True)
        working = working - jnp.dot(low_full, low_full.T, precision=lax.Precision.HIGHEST)
        col_pos = col_ids - first
        in_cols = (col_pos >= 0) & (col_pos < PANEL) & (row_ids >= col_ids)
        col_vals = jnp.take(low_full, jnp.clip(col_pos[0], 0, PANEL - 1), axis=1)
        row_pos = row_ids - first
        in_rows = (row_pos >= 0) & (row_pos < PANEL) & (col_ids > row_ids)
        row_vals = jnp.take(low_full.T, jnp.clip(row_pos[:, 0], 0, PANEL - 1), axis=0)
        packed = packed + jnp.where(in_cols, col_vals, 0.0) + jnp.where(in_rows, row_vals, 0.0)
        covered = covered | in_cols | in_rows
    return jnp.where(covered, packed, working)
```

```python
import jax
import jax.numpy as jnp
from jax import lax
from jax.experimental import pallas as pl
from jax.experimental.pallas import tpu as pltpu
from jax.sharding import PartitionSpec as P

PANEL = 512
PANELS = 2
BASE = 128
FULL = lax.Precision.HIGHEST
HIGH = lax.Precision.HIGH


def gram(left, right):
    return lax.dot_general(
        left, right, (((0,), (0,)), ((), ())), preferred_element_type=jnp.float32
    )


def eliminate(block_ref, inverse_ref):
    tiles = [block_ref[at : at + 8, :] for at in range(0, BASE, 8)]
    lanes = lax.broadcasted_iota(jnp.int32, (8, BASE), 1)
    rows = lax.broadcasted_iota(jnp.int32, (8, BASE), 0)
    for step in range(BASE):
        tile, row = step // 8, step % 8
        own = tiles[tile]
        here = lanes == step
        pivot = jnp.broadcast_to(own[row : row + 1, :], (8, BASE))
        recip = 1.0 / jnp.broadcast_to(pivot[:, step : step + 1], (8, BASE))
        scaled = jnp.where(here, recip, pivot * recip)
        for at in range(tile, BASE // 8):
            if at == tile and row == 7:
                continue
            now = tiles[at]
            factor = jnp.broadcast_to(now[:, step : step + 1], (8, BASE))
            new = jnp.where(here, 0.0, now) - factor * scaled
            tiles[at] = jnp.where(rows > row, new, now) if at == tile else new
    for at, now in enumerate(tiles):
        diag = lanes == rows + 8 * at
        root = lax.rsqrt(jnp.sum(jnp.where(diag, now, 0.0), axis=1, keepdims=True))
        unit = jnp.where(diag, 1.0, jnp.where(lanes < rows + 8 * at, now, 0.0))
        inverse_ref[8 * at : 8 * at + 8, :] = unit * root


def small_inverse(block):
    return pl.pallas_call(
        eliminate,
        out_shape=jax.ShapeDtypeStruct((BASE, BASE), jnp.float32),
        in_specs=[pl.BlockSpec(memory_space=pltpu.VMEM)],
        out_specs=pl.BlockSpec(memory_space=pltpu.VMEM),
        cost_estimate=pl.CostEstimate(
            flops=BASE**3, bytes_accessed=8 * BASE**2, transcendentals=BASE
        ),
        name="eliminate",
    )(block)


def factor_inverse(block):
    size = block.shape[0]
    trailing = block
    inverse = None
    low = []
    for first in range(0, size, BASE):
        diag_inv = small_inverse(trailing[:BASE, :BASE])
        left = jnp.concatenate([c[first - at : first - at + BASE] for at, c in low], axis=1) if low else None
        if inverse is None:
            inverse = diag_inv
        else:
            below = -jnp.dot(
                diag_inv, jnp.dot(left, inverse, precision=FULL), precision=FULL
            )
            inverse = jnp.concatenate(
                [
                    jnp.pad(inverse, ((0, 0), (0, BASE))),
                    jnp.concatenate([below, diag_inv], axis=1),
                ],
                axis=0,
            )
        if first + BASE < size:
            column = lax.dot_general(
                trailing[BASE:, :BASE], diag_inv, (((1,), (1,)), ((), ())), precision=FULL
            )
            low.append((first + BASE, column))
            trailing = trailing[BASE:, BASE:] - lax.dot_general(
                column, column, (((1,), (1,)), ((), ())), precision=FULL
            )
    return inverse


def body(pair_elements, coulomb_root):
    grid_total = coulomb_root.shape[0]
    pairs, grows, gcols = (lax.axis_size(a) for a in ("pair", "grow", "gcol"))
    depth, width = pair_elements.shape
    total = depth * pairs
    tile_rows = grid_total // grows
    tile_cols = grid_total // (gcols * pairs)
    head = PANEL * PANELS
    row_index = lax.axis_index("grow")

    owners = head // width
    parts = grows * gcols
    spread = lax.all_to_all(
        pair_elements.reshape(parts, depth // parts, width), ("grow", "gcol"), 0, 0
    )
    head_el = lax.all_gather(spread[:owners], ("pair", "grow", "gcol"), axis=0)
    head_el = head_el.transpose(0, 2, 1, 3).reshape(total, head)
    head_el, pair_elements = lax.optimization_barrier((head_el, pair_elements))

    row_el = lax.all_gather(pair_elements, ("pair", "gcol"), axis=0)
    row_el = (
        row_el.reshape(pairs, gcols, depth, width)
        .transpose(0, 2, 1, 3)
        .reshape(total, tile_rows)
    )
    share = lax.dynamic_slice_in_dim(
        row_el, lax.axis_index("pair") * tile_cols, tile_cols, 1
    )
    col_el = lax.ppermute(
        share,
        ("grow", "gcol"),
        [(g * gcols + z, z * gcols + g) for g in range(grows) for z in range(gcols)],
    )

    row_base = row_index * tile_rows
    col_tile = lax.axis_index(("gcol", "pair"))
    col_base = col_tile * tile_cols
    scale_head = coulomb_root[:head]
    scale_rows = lax.dynamic_slice_in_dim(coulomb_root, row_base, tile_rows, 0)
    scale_cols = lax.dynamic_slice_in_dim(coulomb_root, col_base, tile_cols, 0)
    row_ids = row_base + jnp.arange(tile_rows, dtype=jnp.int32)[:, None]
    col_ids = col_base + jnp.arange(tile_cols, dtype=jnp.int32)[None, :]
    head_ids = jnp.arange(head, dtype=jnp.int32)

    def dielectric(left, right, left_scale, right_scale, left_ids, right_ids):
        return jnp.where(left_ids == right_ids, 1.0, 0.0).astype(jnp.float32) + (
            left_scale[:, None] * gram(left, right) * right_scale[None, :]
        )

    inverse = factor_inverse(
        dielectric(
            head_el, head_el, scale_head, scale_head, head_ids[:, None], head_ids[None, :]
        )
    )
    panel_cols = dielectric(
        row_el, head_el, scale_rows, scale_head, row_ids, head_ids[None, :]
    )
    panel_rows = dielectric(
        head_el, col_el, scale_head, scale_cols, head_ids[:, None], col_ids
    )
    low_rows = lax.dot_general(
        panel_cols, inverse, (((1,), (1,)), ((), ())), precision=HIGH
    )
    low_cols = jnp.dot(inverse, panel_rows, precision=HIGH)
    working = dielectric(
        row_el, col_el, scale_rows, scale_cols, row_ids, col_ids
    ) - jnp.dot(low_rows, low_cols, precision=HIGH)

    col_vals = lax.dynamic_slice_in_dim(
        low_rows, jnp.minimum(col_base, head - tile_cols), tile_cols, 1
    )
    row_vals = jnp.pad(low_cols, ((0, tile_rows - head), (0, 0)))
    in_cols = (col_ids < head) & (row_ids >= col_ids)
    in_rows = (row_ids < head) & (col_ids > row_ids)
    return jnp.where(in_cols, col_vals, jnp.where(in_rows, row_vals, working))


def solution(mesh):
    return jax.shard_map(
        body,
        mesh=mesh,
        in_specs=(P("pair", ("grow", "gcol")), P()),
        out_specs=P("grow", ("gcol", "pair")),
        check_vma=False,
    )
```
